32 devices in a mesh: groups: 2 (over y), owners: 4 (over z), feat: 2 (over x), rep: 2 (over core).
Axes of the slice: x: 2, y: 2, z: 4, core: 2. Of those that a mesh axis runs over, the one named last changes fastest.
Arguments:
- emb: bfloat16 [16384, 4096], P(('groups', 'owners', 'rep'), 'feat'), parts along dimension 0, as said below
- basis: bfloat16 [4096, 256], P('feat'), may hold values from -0.09375 to 0.09375
- labels: int32 [16384], P(('groups', 'owners', 'rep', 'feat')), parts along dimension 0, may hold values from 0 to 63, as said below
- owner_map: int32 [128], P('groups'), parts along dimension 0, may hold values from 0 to 63, as said below
- order: int32 [16384], P(('groups', 'owners', 'rep', 'feat')), parts along dimension 0, may hold values from 0 to 8191, each once
Outputs:
- best: float32 [16384], P(('groups', 'owners', 'rep', 'feat')), parts along dimension 0
The draws below stay inside these ranges and needn't reach their ends.
There are 2 independent parts, one for each index of `groups`. The reference program is written for one: setup_inputs(seed, part) draws one part's arguments, and reference() takes and returns one part's arrays. A program takes and returns all parts, laid end to end along the dimension named above; an argument that names none is the same for every part. Nothing has to cross between parts.
Inputs may be any that keep to these rules, and one draw needn't show every extreme that they name: `labels`: among the rows of one device at most 128 have slots in one owner column (slot // 8); some owner column receives exactly 128 from every device. `owner_map`: A permutation of the clusters. `emb`: rows cluster around a center of their cluster.
All inputs are finite; a program needn't handle non-finite values.
Results may differ from the reference program's by a relative error of at most 0.0055.
Values may be sent and summed in bfloat16 or wider, within the bound.
A program may use at most 64 MiB of HBM per device.

```python
import jax
import jax.numpy as jnp
from jax import lax

D = 4096
PROJ = 256
ROW_DEV = 512
CL_DEST = 8
ROWS = 8192
NCLUST = 64
CAP = 128
N_OWNERS = 4
N_FEAT = 2
N_REP = 2


def layout(key):
    n_dest = N_OWNERS * N_FEAT
    n_slot = n_dest * CAP
    n_blk = ROWS // ROW_DEV
    heavy = jax.random.randint(jax.random.fold_in(key, 101), (), 0, n_dest)
    idx = jnp.arange(n_slot, dtype=jnp.int32)
    slot_dest = idx // CAP
    scores = jax.random.randint(jax.random.fold_in(key, 102), (n_blk, n_slot), 0, 1 << 20) * n_slot + idx[None, :]
    scores = jnp.where((slot_dest == heavy)[None, :], -1 - idx[None, :], scores)
    picked = jnp.argsort(scores, axis=1)[:, :ROW_DEV]
    dest = slot_dest[picked]
    rows = jnp.arange(ROW_DEV, dtype=jnp.int32)
    mix = jax.random.randint(jax.random.fold_in(key, 103), (n_blk, ROW_DEV), 0, 1 << 20) * ROW_DEV + rows[None, :]
    dest = jnp.take_along_axis(dest, jnp.argsort(mix, axis=1), axis=1)
    first = jax.random.randint(jax.random.fold_in(key, 104), (n_blk, ROW_DEV), 0, CL_DEST)
    second = jax.random.randint(jax.random.fold_in(key, 105), (n_blk, ROW_DEV), 0, CL_DEST)
    slot = dest * CL_DEST + jnp.minimum(first, second)
    owner_map = jax.random.permutation(jax.random.fold_in(key, 106), NCLUST).astype(jnp.int32)
    inverse = jnp.argsort(owner_map).astype(jnp.int32)
    labels = inverse[slot.reshape(ROWS)]
    return (owner_map, labels)


def draw_owner_map(key, part):
    owner_map, labels = layout(key)
    return owner_map


def draw_labels(key, part):
    owner_map, labels = layout(key)
    return labels.astype(jnp.int32)


def draw_emb(key, part):
    owner_map, labels = layout(key)
    key = jax.random.fold_in(key, 7)
    centers = jax.random.normal(jax.random.fold_in(key, 1), (NCLUST, D), jnp.float32)
    noise = jax.random.normal(jax.random.fold_in(key, 2), (ROWS, D), jnp.float32)
    values = centers[labels] + noise
    return values.astype(jnp.bfloat16)


def steps_of(key, extent, split, least, largest):
    loudness = 1.0
    for position, parts in split:
        heights = jax.random.uniform(jax.random.fold_in(jax.random.fold_in(key, 6), position), (parts,), jnp.float32, least / len(split), largest / len(split))
        loudness = loudness * jnp.repeat(jnp.exp(heights), extent[position] // parts).reshape((-1,) + (1,) * (len(extent) - 1 - position))
    return loudness


def bell_draw(key, shape, scale, bound, pieces=(), kind=jnp.bfloat16):
    array = scale * jax.random.normal(key, shape, jnp.float32)
    if pieces:
        array = array * steps_of(key, shape, pieces, -0.22, 0.18)
    return jnp.clip(array, -bound, bound).astype(kind)


def setup_inputs(seed: int = 0, part: int = 0) -> dict:
    streams_of = jax.random.split(jax.random.key(seed), 6)
    part_splits = jax.random.split(jax.random.fold_in(streams_of[5], part), 6)
    emb = draw_emb(jax.random.fold_in(jax.random.fold_in(streams_of[5], part), 71), part)
    basis = bell_draw(streams_of[1], (D, PROJ), D ** -0.5, 0.09375, ((0, 2),))
    labels = draw_labels(jax.random.fold_in(jax.random.fold_in(streams_of[5], part), 71), part)
    owner_map = draw_owner_map(jax.random.fold_in(jax.random.fold_in(streams_of[5], part), 71), part)
    order = jax.random.permutation(part_splits[4], ROWS).astype(jnp.int32)
    return {"emb": emb, "basis": basis, "labels": labels, "owner_map": owner_map, "order": order}


def unitize(diff):
    scale = lax.rsqrt(lax.optimization_barrier(jnp.mean(diff * diff, axis=-1, keepdims=True)) + 1e-06)
    return (diff * scale / jnp.sqrt(jnp.float32(diff.shape[-1]))).astype(jnp.bfloat16)

def reference(emb, basis, labels, owner_map, order):
    proj = jnp.dot(emb, basis, preferred_element_type=jnp.float32).astype(jnp.bfloat16)
    projf = proj.astype(jnp.float32)
    slot = owner_map[labels].astype(jnp.int32)
    sums = jax.ops.segment_sum(projf, slot, num_segments=NCLUST)
    counts = jax.ops.segment_sum(jnp.ones(slot.shape, jnp.float32), slot, num_segments=NCLUST)
    diff = projf - sums[slot] / counts[slot][:, None]
    unit = unitize(diff)
    dest = (slot // CL_DEST).astype(jnp.int32)
    n_dest = NCLUST // CL_DEST
    perm = jnp.argsort(dest, stable=True).astype(jnp.int32)
    dest_count = jax.ops.segment_sum(jnp.ones(dest.shape, jnp.int32), dest, num_segments=n_dest)
    starts = (jnp.cumsum(dest_count) - dest_count).astype(jnp.int32)
    window = N_REP * N_OWNERS * N_FEAT * CAP
    unit_s = jnp.concatenate([unit[perm], jnp.zeros((window, PROJ), jnp.bfloat16)], 0)
    slot_s = jnp.concatenate([slot[perm], -jnp.ones((window,), jnp.int32)], 0)
    order_s = jnp.concatenate([order[perm], jnp.zeros((window,), jnp.int32)], 0)

    def column(d):
        start = starts[d].astype(jnp.int32)
        u = lax.dynamic_slice_in_dim(unit_s, start, window, 0)
        s = lax.dynamic_slice_in_dim(slot_s, start, window, 0)
        o = lax.dynamic_slice_in_dim(order_s, start, window, 0)
        scores = jnp.dot(u, u.T, preferred_element_type=jnp.float32)
        mask = (s[:, None] == s[None, :]) & (o[None, :] < o[:, None]) & (s[None, :] >= 0)
        return lax.optimization_barrier(jnp.max(jnp.where(mask, scores, jnp.float32(-1.0)), axis=1))
    results = lax.map(column, jnp.arange(n_dest, dtype=jnp.int32))
    dest_sorted = dest[perm]
    within = (jnp.arange(ROWS, dtype=jnp.int32) - starts[dest_sorted]).astype(jnp.int32)
    values = results[dest_sorted, within]
    return jnp.zeros((ROWS,), jnp.float32).at[perm].set(values)
```

```python
import functools

import jax
import jax.numpy as jnp
from jax import lax
from jax.experimental import pallas as pl
from jax.experimental.pallas import tpu as pltpu
from jax.sharding import PartitionSpec as P


def unitize(diff):
    scale = lax.rsqrt(jnp.mean(diff * diff, axis=-1, keepdims=True) + 1e-06)
    return (diff * scale / jnp.sqrt(jnp.float32(diff.shape[-1]))).astype(jnp.bfloat16)


def per_device_plain(emb, basis, labels, owner_map, order):
    row_dev = labels.shape[0]
    width = basis.shape[1]
    n_own = lax.axis_size("owners")
    n_col = lax.axis_size("feat")
    n_dest = n_own * n_col
    nclust = owner_map.shape[0]
    cl_dest = nclust // n_dest
    cap = 2 * row_dev // n_dest
    proj = lax.psum_scatter(
        jnp.dot(emb, basis, preferred_element_type=jnp.float32),
        "feat",
        scatter_dimension=0,
        tiled=True,
    ).astype(jnp.bfloat16)
    cluster_ids = jnp.arange(nclust, dtype=jnp.int32)
    slot = jnp.sum(
        jnp.where(labels[:, None] == cluster_ids[None, :], owner_map[None, :], 0), axis=1
    )
    dest = slot // cl_dest
    dest_hot = (dest[:, None] == jnp.arange(n_dest, dtype=jnp.int32)[None, :]).astype(jnp.int32)
    rank = jnp.sum(jnp.cumsum(dest_hot, axis=0) * dest_hot, axis=1) - 1
    place = dest * cap + rank
    member = (slot[:, None] == cluster_ids[None, :]).astype(jnp.bfloat16)
    sums = lax.dot_general(
        member, proj, (((0,), (0,)), ((), ())), preferred_element_type=jnp.float32
    )
    counts = jnp.sum(member.astype(jnp.float32), axis=0)
    all_sums, all_counts = lax.psum((sums, counts), ("owners", "feat", "rep"))
    centre = jnp.take(all_sums, slot, axis=0) / jnp.take(all_counts, slot)[:, None]
    payload = unitize(proj.astype(jnp.float32) - centre)
    vec_buf = jnp.zeros((n_dest * cap, width), jnp.bfloat16).at[place].set(payload)
    slot_buf = jnp.full((n_dest * cap,), -1, jnp.int32).at[place].set(slot)
    order_buf = jnp.zeros((n_dest * cap,), jnp.int32).at[place].set(order)
    got_vec, got_slot, got_order = (
        lax.all_to_all(
            vec_buf.reshape(n_dest, cap, width),
            ("owners", "feat"),
            split_axis=0,
            concat_axis=0,
            tiled=True,
        ),
        lax.all_to_all(
            slot_buf.reshape(n_dest, cap),
            ("owners", "feat"),
            split_axis=0,
            concat_axis=0,
            tiled=True,
        ),
        lax.all_to_all(
            order_buf.reshape(n_dest, cap),
            ("owners", "feat"),
            split_axis=0,
            concat_axis=0,
            tiled=True,
        ),
    )
    held = n_dest * cap
    got_vec = got_vec.reshape(held, width)
    got_slot = got_slot.reshape(held)
    got_order = got_order.reshape(held)
    start_best = jnp.full((held,), -1.0, jnp.float32)
    keys = lax.all_gather(got_vec, "rep", axis=0, tiled=True)
    key_slot = lax.all_gather(got_slot, "rep", axis=0, tiled=True)
    key_order = lax.all_gather(got_order, "rep", axis=0, tiled=True)
    scores = lax.dot_general(
        got_vec, keys, (((1,), (1,)), ((), ())), preferred_element_type=jnp.float32
    )
    mask = (
        (got_slot[:, None] == key_slot[None, :])
        & (key_order[None, :] < got_order[:, None])
        & (key_slot[None, :] >= 0)
    )
    found = jnp.maximum(start_best, jnp.max(jnp.where(mask, scores, jnp.float32(-1.0)), axis=1))
    back = lax.all_to_all(
        found.reshape(n_dest, cap), ("owners", "feat"), split_axis=0, concat_axis=0, tiled=True
    )
    return jnp.take(back.reshape(held), place)


LANES = 128
CHUNKS = 4


def split3(v):
    hi = v.astype(jnp.bfloat16).astype(jnp.float32)
    mid = (v - hi).astype(jnp.bfloat16).astype(jnp.float32)
    return hi, mid, v - hi - mid


def window_kernel(
    n_dest, n_feat, cap,
    emb, basis, labels, owner_map, order, out,
    emb_v, basis_v, own, part_send, part_recv, place_hot, buf, meta_send, meta, rows, unit,
    score_send, back,
    load_sem, part_ssem, part_rsem, meta_ssem, meta_rsem, vec_ssem, vec_rsem,
    fwd_ssem, fwd_rsem, back_ssem, back_rsem,
):
    f32, bf16 = jnp.float32, jnp.bfloat16
    half = part_send.shape[0]
    width = part_send.shape[1]
    held = n_dest * cap
    step = half // CHUNKS
    n_col = width // LANES
    nclust = owner_map.shape[1]
    cl_dest = nclust // n_dest
    feat = lax.axis_index("feat")
    rep = lax.axis_index("rep")
    me = lax.axis_index("owners") * n_feat + feat
    other = 1 - rep

    def device(column, r):
        return {"owners": column // n_feat, "feat": column % n_feat, "rep": r}

    def column_at(k):
        return lax.rem(me + k, n_dest)

    def block(column):
        return pl.ds(pl.multiple_of(column * cap, cap), cap)

    def remote(src, dst, ssem, rsem, to):
        return pltpu.make_async_remote_copy(
            src_ref=src, dst_ref=dst, send_sem=ssem, recv_sem=rsem,
            device_id=to, device_id_type=pl.DeviceIdType.MESH,
        )

    barrier = pltpu.get_barrier_semaphore()
    for k in range(n_dest):
        if k:
            pl.semaphore_signal(barrier, inc=1, device_id=device(column_at(k), rep),
                                device_id_type=pl.DeviceIdType.MESH)
        pl.semaphore_signal(barrier, inc=1, device_id=device(column_at(k), other),
                            device_id_type=pl.DeviceIdType.MESH)

    loads = [pltpu.make_async_copy(basis, basis_v, load_sem.at[2 * CHUNKS])]
    for c in range(2 * CHUNKS):
        side = 1 - feat if c < CHUNKS else feat
        at = pl.multiple_of(side * half + (c % CHUNKS) * step, step)
        loads.append(pltpu.make_async_copy(
            emb.at[pl.ds(at, step), :], emb_v.at[pl.ds(c * step, step), :], load_sem.at[c]))
    for load in loads:
        load.start()

    omap = owner_map[...].astype(f32)
    eye = (lax.broadcasted_iota(jnp.int32, (nclust, nclust), 0)
           == lax.broadcasted_iota(jnp.int32, (nclust, nclust), 1))
    omap_col = jnp.sum(jnp.where(eye, omap, 0.0), axis=1, keepdims=True)
    label_hot = lax.broadcasted_iota(jnp.int32, (nclust, half), 0) == labels[...]
    slot = jnp.sum(jnp.where(label_hot, omap_col, 0.0), axis=0, keepdims=True)
    dest = jnp.floor(slot * (1.0 / cl_dest))
    local = slot - dest * cl_dest
    dest_hot = lax.broadcasted_iota(jnp.int32, (n_dest, half), 0) == dest.astype(jnp.int32)
    upto = (lax.broadcasted_iota(jnp.int32, (half, half), 0)
            <= lax.broadcasted_iota(jnp.int32, (half, half), 1))
    running = jnp.dot(
        jnp.where(dest_hot, 1.0, 0.0).astype(bf16), jnp.where(upto, 1.0, 0.0).astype(bf16),
        preferred_element_type=f32)
    rank = jnp.sum(jnp.where(dest_hot, running, 0.0), axis=0, keepdims=True) - 1.0
    place = (dest * cap + rank).astype(jnp.int32)

    peer = {"feat": 1 - feat}
    part_copies = [[], []]
    loads[0].wait()
    for c in range(CHUNKS):
        at = pl.ds(c * step, step)
        loads[1 + c].wait()
        part_send[at, :] = jnp.dot(
            emb_v[at, :], basis_v[...], preferred_element_type=f32).astype(bf16)
        if c == 0:
            pl.semaphore_wait(barrier, 2 * n_dest - 1)
        cut = (at, pl.ds(0, LANES))
        copy = remote(part_send.at[cut], part_recv.at[cut], part_ssem.at[c], part_rsem.at[c], peer)
        copy.start()
        part_copies[0].append(copy)
    for n in range(1, n_col):
        cut = (slice(None), pl.ds(n * LANES, LANES))
        copy = remote(part_send.at[cut], part_recv.at[cut], part_ssem.at[CHUNKS + n - 1],
                      part_rsem.at[CHUNKS + n - 1], peer)
        copy.start()
        part_copies[n].append(copy)

    place_hot[...] = jnp.where(
        lax.broadcasted_iota(jnp.int32, (held, half), 0) == place, 1.0, 0.0).astype(bf16)
    ranks = order[...]
    pieces = jnp.concatenate([
        local + 1.0,
        lax.shift_right_logical(ranks, 14).astype(f32),
        (lax.shift_right_logical(ranks, 7) & 127).astype(f32),
        (ranks & 127).astype(f32),
        jnp.zeros((4, half), f32)], axis=0).astype(bf16)
    placed = lax.dot_general(pieces, place_hot[...], (((1,), (1,)), ((), ())),
                             preferred_element_type=f32)
    meta_send[...] = jnp.zeros_like(meta_send)
    meta_send[0:1, :] = placed[0:1, :]
    meta_send[1:2, :] = placed[1:2, :] * 16384.0 + placed[2:3, :] * 128.0 + placed[3:4, :]
    meta_copies = []
    for k in range(n_dest):
        to = column_at(k)
        if k:
            meta_copies.append(remote(
                meta_send.at[:, block(to)], meta.at[0, :, block(me)],
                meta_ssem.at[k], meta_rsem.at[k], device(to, rep)))
        meta_copies.append(remote(
            meta_send.at[:, block(to)], meta.at[1, :, block(me)],
            meta_ssem.at[n_dest + k], meta_rsem.at[n_dest + k], device(to, other)))
    for copy in meta_copies:
        copy.start()
    meta[0, :, block(me)] = meta_send[:, block(me)]

    for c in range(CHUNKS):
        at = pl.ds(c * step, step)
        loads[1 + CHUNKS + c].wait()
        own[at, :] = jnp.dot(
            emb_v[pl.ds((CHUNKS + c) * step, step), :], basis_v[...], preferred_element_type=f32)

    vec_copies = [[None] * n_dest for _ in range(n_col)]
    for n in range(n_col):
        lanes = pl.ds(n * LANES, LANES)
        for copy in part_copies[n]:
            copy.wait_recv()
        proj = (own[:, lanes] + part_recv[:, lanes].astype(f32)).astype(bf16)
        buf[:, lanes] = jnp.dot(place_hot[...], proj, preferred_element_type=f32).astype(bf16)
        for k in range(1, n_dest):
            to = column_at(k)
            copy = remote(buf.at[block(to), lanes], rows.at[0, block(me), lanes],
                          vec_ssem.at[n, k], vec_rsem.at[n, k], device(to, rep))
            copy.start()
            vec_copies[n][k] = copy
        rows[0, block(me), lanes] = buf[block(me), lanes]
    for copies in part_copies:
        for copy in copies:
            copy.wait_send()

    for copy in meta_copies:
        copy.wait()
    member = lax.broadcasted_iota(jnp.int32, (8, held), 0).astype(f32) + 1.0
    hot = [jnp.where(meta[r, 0:1, :] == member, 1.0, 0.0) for r in range(2)]
    counts = jnp.sum(hot[0], axis=1, keepdims=True) + jnp.sum(hot[1], axis=1, keepdims=True)
    hot = [h.astype(bf16) for h in hot]

    fwd_copies = []
    for n in range(n_col):
        lanes = pl.ds(n * LANES, LANES)
        for k in range(n_dest):
            came = lax.rem(me + n_dest - k, n_dest)
            if k:
                vec_copies[n][k].wait_recv()
            copy = remote(rows.at[0, block(came), lanes], rows.at[1, block(came), lanes],
                          fwd_ssem.at[n, k], fwd_rsem.at[n, k], {"rep": other})
            copy.start()
            fwd_copies.append(copy)
    sums = jnp.dot(hot[0], rows[0], preferred_element_type=f32)
    for copies in vec_copies:
        for copy in copies[1:]:
            copy.wait_send()
    cols = [jnp.transpose(meta[r]) for r in range(2)]
    for copy in fwd_copies:
        copy.wait()
    sums = sums + jnp.dot(hot[1], rows[1], preferred_element_type=f32)

    centre = jnp.where(counts > 0.0, sums / jnp.maximum(counts, 1.0), 0.0)
    centre3 = jnp.concatenate(
        list(split3(centre)) + [jnp.zeros((LANES - 24, width), f32)], axis=0).astype(bf16)
    lane = lax.broadcasted_iota(jnp.int32, (held, LANES), 1)
    want = jnp.where(lane < 24, (lane & 7) + 1, -1).astype(f32)
    for r in range(2):
        hot_col = jnp.where(cols[r][:, 0:1] == want, 1.0, 0.0).astype(bf16)
        diff = rows[r].astype(f32) - jnp.dot(hot_col, centre3, preferred_element_type=f32)
        mean = jnp.sum(diff * diff, axis=-1, keepdims=True) * (1.0 / width)
        scale = lax.rsqrt(mean + 1e-06)
        unit[r, :, :] = (diff * scale / jnp.sqrt(f32(width))).astype(bf16)

    my_slot, my_order = meta[0, 0:1, :], meta[0, 1:2, :]
    best = jnp.full((1, held), -1.0, f32)
    tile = 256 if held % 256 == 0 else cap
    for r in range(2):
        from_slot = jnp.where(cols[r][:, 0:1] > 0.0, cols[r][:, 0:1], -5.0)
        from_order = cols[r][:, 1:2]
        for t in range(held // tile):
            cut = slice(t * tile, (t + 1) * tile)
            scores = lax.dot_general(unit[r, cut, :], unit[0], (((1,), (1,)), ((), ())),
                                     preferred_element_type=f32)
            mask = (from_slot[cut] == my_slot) & (from_order[cut] < my_order)
            best = jnp.maximum(best, jnp.max(jnp.where(mask, scores, -1.0), axis=0, keepdims=True))

    score_send[...] = jnp.concatenate(list(split3(best)) + [jnp.zeros((5, held), f32)], axis=0)
    back_copies = []
    for k in range(1, n_dest):
        to = column_at(k)
        copy = remote(score_send.at[:, block(to)], back.at[:, block(me)],
                      back_ssem.at[k], back_rsem.at[k], device(to, rep))
        copy.start()
        back_copies.append(copy)
    back[:, block(me)] = score_send[:, block(me)]
    for copy in back_copies:
        copy.wait()
    mine = jnp.dot(back[...].astype(bf16), place_hot[...], preferred_element_type=f32)
    out[...] = mine[0:1, :] + mine[1:2, :] + mine[2:3, :]


def per_device(emb, basis, labels, owner_map, order):
    n_feat = lax.axis_size("feat")
    n_dest = lax.axis_size("owners") * n_feat
    row_dev = labels.shape[0]
    depth, width = basis.shape
    cap = 2 * row_dev // n_dest
    nclust = owner_map.shape[0]
    fits = (
        n_feat == 2 and lax.axis_size("rep") == 2 and cap % LANES == 0 and width == 2 * LANES
        and row_dev % (16 * CHUNKS) == 0 and nclust == 8 * n_dest and n_dest <= 8
    )
    if not fits:
        return per_device_plain(emb, basis, labels, owner_map, order)
    held = n_dest * cap
    n_col = width // LANES
    dma = pltpu.SemaphoreType.DMA
    vmem = pl.BlockSpec(memory_space=pltpu.VMEM)
    hbm = pl.BlockSpec(memory_space=pl.ANY)
    best = pl.pallas_call(
        functools.partial(window_kernel, n_dest, n_feat, cap),
        out_shape=jax.ShapeDtypeStruct((1, row_dev), jnp.float32),
        in_specs=[hbm, hbm, vmem, vmem, vmem],
        out_specs=vmem,
        scratch_shapes=[
            pltpu.VMEM((n_feat * row_dev, depth), jnp.bfloat16),
            pltpu.VMEM((depth, width), jnp.bfloat16),
            pltpu.VMEM((row_dev, width), jnp.float32),
            pltpu.VMEM((row_dev, width), jnp.bfloat16),
            pltpu.VMEM((row_dev, width), jnp.bfloat16),
            pltpu.VMEM((held, row_dev), jnp.bfloat16),
            pltpu.VMEM((held, width), jnp.bfloat16),
            pltpu.VMEM((8, held), jnp.float32),
            pltpu.VMEM((2, 8, held), jnp.float32),
            pltpu.VMEM((2, held, width), jnp.bfloat16),
            pltpu.VMEM((2, held, width), jnp.bfloat16),
            pltpu.VMEM((8, held), jnp.float32),
            pltpu.VMEM((8, held), jnp.float32),
            dma((2 * CHUNKS + 1,)),
            dma((CHUNKS + n_col - 1,)),
            dma((CHUNKS + n_col - 1,)),
            dma((2 * n_dest,)),
            dma((2 * n_dest,)),
            dma((n_col, n_dest)),
            dma((n_col, n_dest)),
            dma((n_col, n_dest)),
            dma((n_col, n_dest)),
            dma((n_dest,)),
            dma((n_dest,)),
        ],
        compiler_params=pltpu.CompilerParams(
            collective_id=0, has_side_effects=True, vmem_limit_bytes=40 * 1024 * 1024
        ),
        name="dedup_window",
    )(emb, basis, labels.reshape(1, row_dev), owner_map.reshape(1, nclust), order.reshape(1, row_dev))
    return best.reshape(row_dev)


def solution(mesh):
    return jax.shard_map(
        per_device,
        mesh=mesh,
        in_specs=(
            P(("groups", "owners", "rep"), "feat"),
            P("feat", None),
            P(("groups", "owners", "rep", "feat")),
            P("groups"),
            P(("groups", "owners", "rep", "feat")),
        ),
        out_specs=P(("groups", "owners", "rep", "feat")),
        check_vma=False,
    )
```

```python
import functools

import jax
import jax.numpy as jnp
from jax import lax
from jax.experimental import pallas as pl
from jax.experimental.pallas import tpu as pltpu
from jax.sharding import PartitionSpec as P


def unitize(diff):
    scale = lax.rsqrt(jnp.mean(diff * diff, axis=-1, keepdims=True) + 1e-06)
    return (diff * scale / jnp.sqrt(jnp.float32(diff.shape[-1]))).astype(jnp.bfloat16)


def per_device_plain(emb, basis, labels, owner_map, order):
    row_dev = labels.shape[0]
    width = basis.shape[1]
    n_own = lax.axis_size("owners")
    n_col = lax.axis_size("feat")
    n_dest = n_own * n_col
    nclust = owner_map.shape[0]
    cl_dest = nclust // n_dest
    cap = 2 * row_dev // n_dest
    proj = lax.psum_scatter(
        jnp.dot(emb, basis, preferred_element_type=jnp.float32),
        "feat",
        scatter_dimension=0,
        tiled=True,
    ).astype(jnp.bfloat16)
    cluster_ids = jnp.arange(nclust, dtype=jnp.int32)
    slot = jnp.sum(
        jnp.where(labels[:, None] == cluster_ids[None, :], owner_map[None, :], 0), axis=1
    )
    dest = slot // cl_dest
    dest_hot = (dest[:, None] == jnp.arange(n_dest, dtype=jnp.int32)[None, :]).astype(jnp.int32)
    rank = jnp.sum(jnp.cumsum(dest_hot, axis=0) * dest_hot, axis=1) - 1
    place = dest * cap + rank
    member = (slot[:, None] == cluster_ids[None, :]).astype(jnp.bfloat16)
    sums = lax.dot_general(
        member, proj, (((0,), (0,)), ((), ())), preferred_element_type=jnp.float32
    )
    counts = jnp.sum(member.astype(jnp.float32), axis=0)
    all_sums, all_counts = lax.psum((sums, counts), ("owners", "feat", "rep"))
    centre = jnp.take(all_sums, slot, axis=0) / jnp.take(all_counts, slot)[:, None]
    payload = unitize(proj.astype(jnp.float32) - centre)
    vec_buf = jnp.zeros((n_dest * cap, width), jnp.bfloat16).at[place].set(payload)
    slot_buf = jnp.full((n_dest * cap,), -1, jnp.int32).at[place].set(slot)
    order_buf = jnp.zeros((n_dest * cap,), jnp.int32).at[place].set(order)
    got_vec, got_slot, got_order = (
        lax.all_to_all(
            vec_buf.reshape(n_dest, cap, width),
            ("owners", "feat"),
            split_axis=0,
            concat_axis=0,
            tiled=True,
        ),
        lax.all_to_all(
            slot_buf.reshape(n_dest, cap),
            ("owners", "feat"),
            split_axis=0,
            concat_axis=0,
            tiled=True,
        ),
        lax.all_to_all(
            order_buf.reshape(n_dest, cap),
            ("owners", "feat"),
            split_axis=0,
            concat_axis=0,
            tiled=True,
        ),
    )
    held = n_dest * cap
    got_vec = got_vec.reshape(held, width)
    got_slot = got_slot.reshape(held)
    got_order = got_order.reshape(held)
    start_best = jnp.full((held,), -1.0, jnp.float32)
    keys = lax.all_gather(got_vec, "rep", axis=0, tiled=True)
    key_slot = lax.all_gather(got_slot, "rep", axis=0, tiled=True)
    key_order = lax.all_gather(got_order, "rep", axis=0, tiled=True)
    scores = lax.dot_general(
        got_vec, keys, (((1,), (1,)), ((), ())), preferred_element_type=jnp.float32
    )
    mask = (
        (got_slot[:, None] == key_slot[None, :])
        & (key_order[None, :] < got_order[:, None])
        & (key_slot[None, :] >= 0)
    )
    found = jnp.maximum(start_best, jnp.max(jnp.where(mask, scores, jnp.float32(-1.0)), axis=1))
    back = lax.all_to_all(
        found.reshape(n_dest, cap), ("owners", "feat"), split_axis=0, concat_axis=0, tiled=True
    )
    return jnp.take(back.reshape(held), place)


LANES = 128
CHUNKS = 4


def split3(v):
    hi = v.astype(jnp.bfloat16).astype(jnp.float32)
    mid = (v - hi).astype(jnp.bfloat16).astype(jnp.float32)
    return hi, mid, v - hi - mid


def window_kernel(
    n_dest, n_feat, cap,
    emb, basis, labels_h, owner_map_h, order_h, out,
    labels, owner_map, order, emb_v, basis_v, own, part_send, part_recv, place_hot, buf, meta_send, meta, rows, unit,
    score_send, back,
    load_sem, part_ssem, part_rsem, meta_ssem, meta_rsem, vec_ssem, vec_rsem,
    fwd_ssem, fwd_rsem, back_ssem, back_rsem,
):
    f32, bf16 = jnp.float32, jnp.bfloat16
    half = part_send.shape[0]
    width = part_send.shape[1]
    held = n_dest * cap
    step = half // CHUNKS
    n_col = width // LANES
    nclust = owner_map.shape[1]
    cl_dest = nclust // n_dest
    feat = lax.axis_index("feat")
    rep = lax.axis_index("rep")
    me = lax.axis_index("owners") * n_feat + feat
    other = 1 - rep

    def device(column, r):
        return {"owners": column // n_feat, "feat": column % n_feat, "rep": r}

    def column_at(k):
        return lax.rem(me + k, n_dest)

    def block(column):
        return pl.ds(pl.multiple_of(column * cap, cap), cap)

    def remote(src, dst, ssem, rsem, to):
        return pltpu.make_async_remote_copy(
            src_ref=src, dst_ref=dst, send_sem=ssem, recv_sem=rsem,
            device_id=to, device_id_type=pl.DeviceIdType.MESH,
        )

    barrier = pltpu.get_barrier_semaphore()
    for k in range(n_dest):
        if k:
            pl.semaphore_signal(barrier, inc=1, device_id=device(column_at(k), rep),
                                device_id_type=pl.DeviceIdType.MESH)
        pl.semaphore_signal(barrier, inc=1, device_id=device(column_at(k), other),
                            device_id_type=pl.DeviceIdType.MESH)

    small = [pltpu.make_async_copy(h, v, load_sem.at[2 * CHUNKS + 1 + i]) for i, (h, v) in enumerate(
        ((labels_h, labels), (owner_map_h, owner_map), (order_h, order)))]
    loads = [pltpu.make_async_copy(basis, basis_v, load_sem.at[2 * CHUNKS])]
    for c in range(2 * CHUNKS):
        side = 1 - feat if c < CHUNKS else feat
        at = pl.multiple_of(side * half + (c % CHUNKS) * step, step)
        loads.append(pltpu.make_async_copy(
            emb.at[pl.ds(at, step), :], emb_v.at[pl.ds(c * step, step), :], load_sem.at[c]))
    for load in small + loads:
        load.start()

    for load in small:
        load.wait()
    omap = owner_map[...].astype(f32)
    eye = (lax.broadcasted_iota(jnp.int32, (nclust, nclust), 0)
           == lax.broadcasted_iota(jnp.int32, (nclust, nclust), 1))
    omap_col = jnp.sum(jnp.where(eye, omap, 0.0), axis=1, keepdims=True)
    label_hot = lax.broadcasted_iota(jnp.int32, (nclust, half), 0) == labels[...]
    slot = jnp.sum(jnp.where(label_hot, omap_col, 0.0), axis=0, keepdims=True)
    dest = jnp.floor(slot * (1.0 / cl_dest))
    local = slot - dest * cl_dest
    dest_hot = lax.broadcasted_iota(jnp.int32, (n_dest, half), 0) == dest.astype(jnp.int32)
    upto = (lax.broadcasted_iota(jnp.int32, (half, half), 0)
            <= lax.broadcasted_iota(jnp.int32, (half, half), 1))
    running = jnp.dot(
        jnp.where(dest_hot, 1.0, 0.0).astype(bf16), jnp.where(upto, 1.0, 0.0).astype(bf16),
        preferred_element_type=f32)
    rank = jnp.sum(jnp.where(dest_hot, running, 0.0), axis=0, keepdims=True) - 1.0
    place = (dest * cap + rank).astype(jnp.int32)

    peer = {"feat": 1 - feat}
    part_copies = [[], []]
    loads[0].wait()
    for c in range(CHUNKS):
        at = pl.ds(c * step, step)
        loads[1 + c].wait()
        part_send[at, :] = jnp.dot(
            emb_v[at, :], basis_v[...], preferred_element_type=f32).astype(bf16)
        if c == 0:
            pl.semaphore_wait(barrier, 2 * n_dest - 1)
        cut = (at, pl.ds(0, LANES))
        copy = remote(part_send.at[cut], part_recv.at[cut], part_ssem.at[c], part_rsem.at[c], peer)
        copy.start()
        part_copies[0].append(copy)
    for n in range(1, n_col):
        cut = (slice(None), pl.ds(n * LANES, LANES))
        copy = remote(part_send.at[cut], part_recv.at[cut], part_ssem.at[CHUNKS + n - 1],
                      part_rsem.at[CHUNKS + n - 1], peer)
        copy.start()
        part_copies[n].append(copy)

    place_hot[...] = jnp.where(
        lax.broadcasted_iota(jnp.int32, (held, half), 0) == place, 1.0, 0.0).astype(bf16)
    ranks = order[...]
    pieces = jnp.concatenate([
        local + 1.0,
        lax.shift_right_logical(ranks, 14).astype(f32),
        (lax.shift_right_logical(ranks, 7) & 127).astype(f32),
        (ranks & 127).astype(f32),
        jnp.zeros((4, half), f32)], axis=0).astype(bf16)
    placed = lax.dot_general(pieces, place_hot[...], (((1,), (1,)), ((), ())),
                             preferred_element_type=f32)
    meta_send[...] = jnp.zeros_like(meta_send)
    meta_send[0:1, :] = placed[0:1, :]
    meta_send[1:2, :] = placed[1:2, :] * 16384.0 + placed[2:3, :] * 128.0 + placed[3:4, :]
    meta_copies = []
    for k in range(n_dest):
        to = column_at(k)
        if k:
            meta_copies.append(remote(
                meta_send.at[:, block(to)], meta.at[0, :, block(me)],
                meta_ssem.at[k], meta_rsem.at[k], device(to, rep)))
        meta_copies.append(remote(
            meta_send.at[:, block(to)], meta.at[1, :, block(me)],
            meta_ssem.at[n_dest + k], meta_rsem.at[n_dest + k], device(to, other)))
    for copy in meta_copies:
        copy.start()
    meta[0, :, block(me)] = meta_send[:, block(me)]

    for c in range(CHUNKS):
        at = pl.ds(c * step, step)
        loads[1 + CHUNKS + c].wait()
        own[at, :] = jnp.dot(
            emb_v[pl.ds((CHUNKS + c) * step, step), :], basis_v[...], preferred_element_type=f32)

    vec_copies = [[None] * n_dest for _ in range(n_col)]
    for n in range(n_col):
        lanes = pl.ds(n * LANES, LANES)
        for copy in part_copies[n]:
            copy.wait_recv()
        proj = (own[:, lanes] + part_recv[:, lanes].astype(f32)).astype(bf16)
        buf[:, lanes] = jnp.dot(place_hot[...], proj, preferred_element_type=f32).astype(bf16)
        for k in range(1, n_dest):
            to = column_at(k)
            copy = remote(buf.at[block(to), lanes], rows.at[0, block(me), lanes],
                          vec_ssem.at[n, k], vec_rsem.at[n, k], device(to, rep))
            copy.start()
            vec_copies[n][k] = copy
        rows[0, block(me), lanes] = buf[block(me), lanes]
    for copies in part_copies:
        for copy in copies:
            copy.wait_send()

    for copy in meta_copies:
        copy.wait()
    member = lax.broadcasted_iota(jnp.int32, (8, held), 0).astype(f32) + 1.0
    hot = [jnp.where(meta[r, 0:1, :] == member, 1.0, 0.0) for r in range(2)]
    counts = jnp.sum(hot[0], axis=1, keepdims=True) + jnp.sum(hot[1], axis=1, keepdims=True)
    hot = [h.astype(bf16) for h in hot]

    fwd_copies = []
    for n in range(n_col):
        lanes = pl.ds(n * LANES, LANES)
        for k in range(n_dest):
            came = lax.rem(me + n_dest - k, n_dest)
            if k:
                vec_copies[n][k].wait_recv()
            copy = remote(rows.at[0, block(came), lanes], rows.at[1, block(came), lanes],
                          fwd_ssem.at[n, k], fwd_rsem.at[n, k], {"rep": other})
            copy.start()
            fwd_copies.append(copy)
    sums = jnp.dot(hot[0], rows[0], preferred_element_type=f32)
    for copies in vec_copies:
        for copy in copies[1:]:
            copy.wait_send()
    cols = [jnp.transpose(meta[r]) for r in range(2)]
    for copy in fwd_copies:
        copy.wait()
    sums = sums + jnp.dot(hot[1], rows[1], preferred_element_type=f32)

    centre = jnp.where(counts > 0.0, sums / jnp.maximum(counts, 1.0), 0.0)
    centre3 = jnp.concatenate(
        list(split3(centre)) + [jnp.zeros((LANES - 24, width), f32)], axis=0).astype(bf16)
    lane = lax.broadcasted_iota(jnp.int32, (held, LANES), 1)
    want = jnp.where(lane < 24, (lane & 7) + 1, -1).astype(f32)
    for r in range(2):
        hot_col = jnp.where(cols[r][:, 0:1] == want, 1.0, 0.0).astype(bf16)
        diff = rows[r].astype(f32) - jnp.dot(hot_col, centre3, preferred_element_type=f32)
        mean = jnp.sum(diff * diff, axis=-1, keepdims=True) * (1.0 / width)
        scale = lax.rsqrt(mean + 1e-06)
        unit[r, :, :] = (diff * scale / jnp.sqrt(f32(width))).astype(bf16)

    my_slot, my_order = meta[0, 0:1, :], meta[0, 1:2, :]
    best = jnp.full((1, held), -1.0, f32)
    tile = 256 if held % 256 == 0 else cap
    for r in range(2):
        from_slot = jnp.where(cols[r][:, 0:1] > 0.0, cols[r][:, 0:1], -5.0)
        from_order = cols[r][:, 1:2]
        for t in range(held // tile):
            cut = slice(t * tile, (t + 1) * tile)
            scores = lax.dot_general(unit[r, cut, :], unit[0], (((1,), (1,)), ((), ())),
                                     preferred_element_type=f32)
            mask = (from_slot[cut] == my_slot) & (from_order[cut] < my_order)
            best = jnp.maximum(best, jnp.max(jnp.where(mask, scores, -1.0), axis=0, keepdims=True))

    score_send[...] = jnp.concatenate(list(split3(best)) + [jnp.zeros((5, held), f32)], axis=0)
    back_copies = []
    for k in range(1, n_dest):
        to = column_at(k)
        copy = remote(score_send.at[:, block(to)], back.at[:, block(me)],
                      back_ssem.at[k], back_rsem.at[k], device(to, rep))
        copy.start()
        back_copies.append(copy)
    back[:, block(me)] = score_send[:, block(me)]
    for copy in back_copies:
        copy.wait()
    mine = jnp.dot(back[...].astype(bf16), place_hot[...], preferred_element_type=f32)
    out[...] = mine[0:1, :] + mine[1:2, :] + mine[2:3, :]


def per_device(emb, basis, labels, owner_map, order):
    n_feat = lax.axis_size("feat")
    n_dest = lax.axis_size("owners") * n_feat
    row_dev = labels.shape[0]
    depth, width = basis.shape
    cap = 2 * row_dev // n_dest
    nclust = owner_map.shape[0]
    fits = (
        n_feat == 2 and lax.axis_size("rep") == 2 and cap % LANES == 0 and width == 2 * LANES
        and row_dev % (16 * CHUNKS) == 0 and nclust == 8 * n_dest and n_dest <= 8
    )
    if not fits:
        return per_device_plain(emb, basis, labels, owner_map, order)
    held = n_dest * cap
    n_col = width // LANES
    dma = pltpu.SemaphoreType.DMA
    vmem = pl.BlockSpec(memory_space=pltpu.VMEM)
    hbm = pl.BlockSpec(memory_space=pltpu.HBM)
    best = pl.pallas_call(
        functools.partial(window_kernel, n_dest, n_feat, cap),
        out_shape=jax.ShapeDtypeStruct((1, row_dev), jnp.float32),
        in_specs=[hbm] * 5,
        out_specs=vmem,
        scratch_shapes=[
            pltpu.VMEM((1, row_dev), jnp.int32),
            pltpu.VMEM((1, nclust), jnp.int32),
            pltpu.VMEM((1, row_dev), jnp.int32),
            pltpu.VMEM((n_feat * row_dev, depth), jnp.bfloat16),
            pltpu.VMEM((depth, width), jnp.bfloat16),
            pltpu.VMEM((row_dev, width), jnp.float32),
            pltpu.VMEM((row_dev, width), jnp.bfloat16),
            pltpu.VMEM((row_dev, width), jnp.bfloat16),
            pltpu.VMEM((held, row_dev), jnp.bfloat16),
            pltpu.VMEM((held, width), jnp.bfloat16),
            pltpu.VMEM((8, held), jnp.float32),
            pltpu.VMEM((2, 8, held), jnp.float32),
            pltpu.VMEM((2, held, width), jnp.bfloat16),
            pltpu.VMEM((2, held, width), jnp.bfloat16),
            pltpu.VMEM((8, held), jnp.float32),
            pltpu.VMEM((8, held), jnp.float32),
            dma((2 * CHUNKS + 4,)),
            dma((CHUNKS + n_col - 1,)),
            dma((CHUNKS + n_col - 1,)),
            dma((2 * n_dest,)),
            dma((2 * n_dest,)),
            dma((n_col, n_dest)),
            dma((n_col, n_dest)),
            dma((n_col, n_dest)),
            dma((n_col, n_dest)),
            dma((n_dest,)),
            dma((n_dest,)),
        ],
        compiler_params=pltpu.CompilerParams(
            collective_id=0, has_side_effects=True, vmem_limit_bytes=60 * 1024 * 1024
        ),
        name="dedup_window",
    )(emb, basis, labels.reshape(1, row_dev), owner_map.reshape(1, nclust), order.reshape(1, row_dev))
    return best.reshape(row_dev)


def solution(mesh):
    return jax.shard_map(
        per_device,
        mesh=mesh,
        in_specs=(
            P(("groups", "owners", "rep"), "feat"),
            P("feat", None),
            P(("groups", "owners", "rep", "feat")),
            P("groups"),
            P(("groups", "owners", "rep", "feat")),
        ),
        out_specs=P(("groups", "owners", "rep", "feat")),
        check_vma=False,
    )
```

```python
import functools

import jax
import jax.numpy as jnp
from jax import lax
from jax.experimental import pallas as pl
from jax.experimental.pallas import tpu as pltpu
from jax.sharding import PartitionSpec as P


def unitize(diff):
    scale = lax.rsqrt(jnp.mean(diff * diff, axis=-1, keepdims=True) + 1e-06)
    return (diff * scale / jnp.sqrt(jnp.float32(diff.shape[-1]))).astype(jnp.bfloat16)


def per_device_plain(emb, basis, labels, owner_map, order):
    row_dev = labels.shape[0]
    width = basis.shape[1]
    n_own = lax.axis_size("owners")
    n_col = lax.axis_size("feat")
    n_dest = n_own * n_col
    nclust = owner_map.shape[0]
    cl_dest = nclust // n_dest
    cap = 2 * row_dev // n_dest
    proj = lax.psum_scatter(
        jnp.dot(emb, basis, preferred_element_type=jnp.float32),
        "feat",
        scatter_dimension=0,
        tiled=True,
    ).astype(jnp.bfloat16)
    cluster_ids = jnp.arange(nclust, dtype=jnp.int32)
    slot = jnp.sum(
        jnp.where(labels[:, None] == cluster_ids[None, :], owner_map[None, :], 0), axis=1
    )
    dest = slot // cl_dest
    dest_hot = (dest[:, None] == jnp.arange(n_dest, dtype=jnp.int32)[None, :]).astype(jnp.int32)
    rank = jnp.sum(jnp.cumsum(dest_hot, axis=0) * dest_hot, axis=1) - 1
    place = dest * cap + rank
    member = (slot[:, None] == cluster_ids[None, :]).astype(jnp.bfloat16)
    sums = lax.dot_general(
        member, proj, (((0,), (0,)), ((), ())), preferred_element_type=jnp.float32
    )
    counts = jnp.sum(member.astype(jnp.float32), axis=0)
    all_sums, all_counts = lax.psum((sums, counts), ("owners", "feat", "rep"))
    centre = jnp.take(all_sums, slot, axis=0) / jnp.take(all_counts, slot)[:, None]
    payload = unitize(proj.astype(jnp.float32) - centre)
    vec_buf = jnp.zeros((n_dest * cap, width), jnp.bfloat16).at[place].set(payload)
    slot_buf = jnp.full((n_dest * cap,), -1, jnp.int32).at[place].set(slot)
    order_buf = jnp.zeros((n_dest * cap,), jnp.int32).at[place].set(order)
    got_vec, got_slot, got_order = (
        lax.all_to_all(
            vec_buf.reshape(n_dest, cap, width),
            ("owners", "feat"),
            split_axis=0,
            concat_axis=0,
            tiled=True,
        ),
        lax.all_to_all(
            slot_buf.reshape(n_dest, cap),
            ("owners", "feat"),
            split_axis=0,
            concat_axis=0,
            tiled=True,
        ),
        lax.all_to_all(
            order_buf.reshape(n_dest, cap),
            ("owners", "feat"),
            split_axis=0,
            concat_axis=0,
            tiled=True,
        ),
    )
    held = n_dest * cap
    got_vec = got_vec.reshape(held, width)
    got_slot = got_slot.reshape(held)
    got_order = got_order.reshape(held)
    start_best = jnp.full((held,), -1.0, jnp.float32)
    keys = lax.all_gather(got_vec, "rep", axis=0, tiled=True)
    key_slot = lax.all_gather(got_slot, "rep", axis=0, tiled=True)
    key_order = lax.all_gather(got_order, "rep", axis=0, tiled=True)
    scores = lax.dot_general(
        got_vec, keys, (((1,), (1,)), ((), ())), preferred_element_type=jnp.float32
    )
    mask = (
        (got_slot[:, None] == key_slot[None, :])
        & (key_order[None, :] < got_order[:, None])
        & (key_slot[None, :] >= 0)
    )
    found = jnp.maximum(start_best, jnp.max(jnp.where(mask, scores, jnp.float32(-1.0)), axis=1))
    back = lax.all_to_all(
        found.reshape(n_dest, cap), ("owners", "feat"), split_axis=0, concat_axis=0, tiled=True
    )
    return jnp.take(back.reshape(held), place)


LANES = 128
CHUNKS = 4


def split3(v):
    hi = v.astype(jnp.bfloat16).astype(jnp.float32)
    mid = (v - hi).astype(jnp.bfloat16).astype(jnp.float32)
    return hi, mid, v - hi - mid


def window_kernel(
    n_dest, n_feat, cap,
    emb, basis, labels_h, owner_map_h, order_h, out,
    labels, owner_map, order, emb_v, basis_v, own, part_send, part_recv, place_hot, buf, meta_send, meta, rows, unit,
    score_send, back,
    near_sem, load_sem, part_ssem, part_rsem, meta_ssem, meta_rsem, vec_ssem, vec_rsem,
    fwd_ssem, fwd_rsem, back_ssem, back_rsem,
):
    f32, bf16 = jnp.float32, jnp.bfloat16
    half = part_send.shape[0]
    width = part_send.shape[1]
    held = n_dest * cap
    step = half // CHUNKS
    n_col = width // LANES
    nclust = owner_map.shape[1]
    cl_dest = nclust // n_dest
    feat = lax.axis_index("feat")
    rep = lax.axis_index("rep")
    me = lax.axis_index("owners") * n_feat + feat
    other = 1 - rep

    def device(column, r):
        return {"owners": column // n_feat, "feat": column % n_feat, "rep": r}

    def column_at(k):
        return lax.rem(me + k, n_dest)

    def block(column):
        return pl.ds(pl.multiple_of(column * cap, cap), cap)

    def remote(src, dst, ssem, rsem, to):
        return pltpu.make_async_remote_copy(
            src_ref=src, dst_ref=dst, send_sem=ssem, recv_sem=rsem,
            device_id=to, device_id_type=pl.DeviceIdType.MESH,
        )

    barrier = pltpu.get_barrier_semaphore()
    owner = lax.axis_index("owners")
    n_own = n_dest // n_feat
    low, high = owner > 0, owner < n_own - 1
    n_near = 1 + low.astype(jnp.int32) + high.astype(jnp.int32)

    def greet(sem):
        def signal(to):
            pl.semaphore_signal(sem, inc=1, device_id=to, device_id_type=pl.DeviceIdType.MESH)

        signal({"feat": 1 - feat})

        @pl.when(low)
        def _():
            signal({"owners": owner - 1})

        @pl.when(high)
        def _():
            signal({"owners": owner + 1})

    greet(barrier)
    pl.semaphore_signal(barrier, inc=1, device_id={"rep": other}, device_id_type=pl.DeviceIdType.MESH)

    small = [pltpu.make_async_copy(h, v, load_sem.at[2 * CHUNKS + 1 + i]) for i, (h, v) in enumerate(
        ((labels_h, labels), (owner_map_h, owner_map), (order_h, order)))]
    loads = [pltpu.make_async_copy(basis, basis_v, load_sem.at[2 * CHUNKS])]
    for c in range(2 * CHUNKS):
        side = 1 - feat if c < CHUNKS else feat
        at = pl.multiple_of(side * half + (c % CHUNKS) * step, step)
        loads.append(pltpu.make_async_copy(
            emb.at[pl.ds(at, step), :], emb_v.at[pl.ds(c * step, step), :], load_sem.at[c]))
    for load in small + loads:
        load.start()

    for load in small:
        load.wait()
    omap = owner_map[...].astype(f32)
    eye = (lax.broadcasted_iota(jnp.int32, (nclust, nclust), 0)
           == lax.broadcasted_iota(jnp.int32, (nclust, nclust), 1))
    omap_col = jnp.sum(jnp.where(eye, omap, 0.0), axis=1, keepdims=True)
    label_hot = lax.broadcasted_iota(jnp.int32, (nclust, half), 0) == labels[...]
    slot = jnp.sum(jnp.where(label_hot, omap_col, 0.0), axis=0, keepdims=True)
    dest = jnp.floor(slot * (1.0 / cl_dest))
    local = slot - dest * cl_dest
    dest_hot = lax.broadcasted_iota(jnp.int32, (n_dest, half), 0) == dest.astype(jnp.int32)
    upto = (lax.broadcasted_iota(jnp.int32, (half, half), 0)
            <= lax.broadcasted_iota(jnp.int32, (half, half), 1))
    running = jnp.dot(
        jnp.where(dest_hot, 1.0, 0.0).astype(bf16), jnp.where(upto, 1.0, 0.0).astype(bf16),
        preferred_element_type=f32)
    rank = jnp.sum(jnp.where(dest_hot, running, 0.0), axis=0, keepdims=True) - 1.0
    place = (dest * cap + rank).astype(jnp.int32)

    peer = {"feat": 1 - feat}
    part_copies = [[], []]
    loads[0].wait()
    for c in range(CHUNKS):
        at = pl.ds(c * step, step)
        loads[1 + c].wait()
        part_send[at, :] = jnp.dot(
            emb_v[at, :], basis_v[...], preferred_element_type=f32).astype(bf16)
        if c == 0:
            pl.semaphore_wait(barrier, 1 + n_near)
            greet(near_sem.at[0])
        cut = (at, pl.ds(0, LANES))
        copy = remote(part_send.at[cut], part_recv.at[cut], part_ssem.at[c], part_rsem.at[c], peer)
        copy.start()
        part_copies[0].append(copy)
    for n in range(1, n_col):
        cut = (slice(None), pl.ds(n * LANES, LANES))
        copy = remote(part_send.at[cut], part_recv.at[cut], part_ssem.at[CHUNKS + n - 1],
                      part_rsem.at[CHUNKS + n - 1], peer)
        copy.start()
        part_copies[n].append(copy)

    def hear(c):
        pl.semaphore_wait(near_sem.at[c], n_near)
        if c < n_own - 2:
            greet(near_sem.at[c + 1])

    hear(0)

    place_hot[...] = jnp.where(
        lax.broadcasted_iota(jnp.int32, (held, half), 0) == place, 1.0, 0.0).astype(bf16)
    ranks = order[...]
    pieces = jnp.concatenate([
        local + 1.0,
        lax.shift_right_logical(ranks, 14).astype(f32),
        (lax.shift_right_logical(ranks, 7) & 127).astype(f32),
        (ranks & 127).astype(f32),
        jnp.zeros((4, half), f32)], axis=0).astype(bf16)
    placed = lax.dot_general(pieces, place_hot[...], (((1,), (1,)), ((), ())),
                             preferred_element_type=f32)
    meta_send[...] = jnp.zeros_like(meta_send)
    meta_send[0:1, :] = placed[0:1, :]
    meta_send[1:2, :] = placed[1:2, :] * 16384.0 + placed[2:3, :] * 128.0 + placed[3:4, :]
    hear(1)

    for c in range(CHUNKS):
        at = pl.ds(c * step, step)
        loads[1 + CHUNKS + c].wait()
        own[at, :] = jnp.dot(
            emb_v[pl.ds((CHUNKS + c) * step, step), :], basis_v[...], preferred_element_type=f32)

    hear(2)
    meta_copies = [None]
    for k in range(1, n_dest):
        to = column_at(k)
        copy = remote(meta_send.at[:, block(to)], meta.at[0, :, block(me)],
                      meta_ssem.at[k], meta_rsem.at[k], device(to, rep))
        copy.start()
        meta_copies.append(copy)
    meta[0, :, block(me)] = meta_send[:, block(me)]

    order_of_sends = sorted(range(1, n_dest), key=lambda k: -min(k, n_dest - k))

    vec_copies = [[None] * n_dest for _ in range(n_col)]
    for n in range(n_col):
        lanes = pl.ds(n * LANES, LANES)
        for copy in part_copies[n]:
            copy.wait_recv()
        proj = (own[:, lanes] + part_recv[:, lanes].astype(f32)).astype(bf16)
        buf[:, lanes] = jnp.dot(place_hot[...], proj, preferred_element_type=f32).astype(bf16)
        for k in order_of_sends:
            to = column_at(k)
            copy = remote(buf.at[block(to), lanes], rows.at[0, block(me), lanes],
                          vec_ssem.at[n, k], vec_rsem.at[n, k], device(to, rep))
            copy.start()
            vec_copies[n][k] = copy
        rows[0, block(me), lanes] = buf[block(me), lanes]
    for copies in part_copies:
        for copy in copies:
            copy.wait_send()

    for copy in meta_copies[1:]:
        copy.wait()
    copy = remote(meta.at[0], meta.at[1], meta_ssem.at[0], meta_rsem.at[0], {"rep": other})
    copy.start()
    copy.wait()
    member = lax.broadcasted_iota(jnp.int32, (8, held), 0).astype(f32) + 1.0
    hot = [jnp.where(meta[r, 0:1, :] == member, 1.0, 0.0) for r in range(2)]
    counts = jnp.sum(hot[0], axis=1, keepdims=True) + jnp.sum(hot[1], axis=1, keepdims=True)
    hot = [h.astype(bf16) for h in hot]

    fwd_copies = []
    for n in range(n_col):
        lanes = pl.ds(n * LANES, LANES)
        for k in range(n_dest):
            came = lax.rem(me + n_dest - k, n_dest)
            if k:
                vec_copies[n][k].wait_recv()
            copy = remote(rows.at[0, block(came), lanes], rows.at[1, block(came), lanes],
                          fwd_ssem.at[n, k], fwd_rsem.at[n, k], {"rep": other})
            copy.start()
            fwd_copies.append(copy)
    sums = jnp.dot(hot[0], rows[0], preferred_element_type=f32)
    for copies in vec_copies:
        for copy in copies[1:]:
            copy.wait_send()
    cols = [jnp.transpose(meta[r]) for r in range(2)]
    for copy in fwd_copies:
        copy.wait()
    sums = sums + jnp.dot(hot[1], rows[1], preferred_element_type=f32)

    centre = jnp.where(counts > 0.0, sums / jnp.maximum(counts, 1.0), 0.0)
    centre3 = jnp.concatenate(
        list(split3(centre)) + [jnp.zeros((LANES - 24, width), f32)], axis=0).astype(bf16)
    lane = lax.broadcasted_iota(jnp.int32, (held, LANES), 1)
    want = jnp.where(lane < 24, (lane & 7) + 1, -1).astype(f32)
    for r in range(2):
        hot_col = jnp.where(cols[r][:, 0:1] == want, 1.0, 0.0).astype(bf16)
        diff = rows[r].astype(f32) - jnp.dot(hot_col, centre3, preferred_element_type=f32)
        mean = jnp.sum(diff * diff, axis=-1, keepdims=True) * (1.0 / width)
        scale = lax.rsqrt(mean + 1e-06)
        unit[r, :, :] = (diff * scale / jnp.sqrt(f32(width))).astype(bf16)

    my_slot, my_order = meta[0, 0:1, :], meta[0, 1:2, :]
    best = jnp.full((1, held), -1.0, f32)
    tile = 256 if held % 256 == 0 else cap
    for r in range(2):
        from_slot = jnp.where(cols[r][:, 0:1] > 0.0, cols[r][:, 0:1], -5.0)
        from_order = cols[r][:, 1:2]
        for t in range(held // tile):
            cut = slice(t * tile, (t + 1) * tile)
            scores = lax.dot_general(unit[r, cut, :], unit[0], (((1,), (1,)), ((), ())),
                                     preferred_element_type=f32)
            mask = (from_slot[cut] == my_slot) & (from_order[cut] < my_order)
            best = jnp.maximum(best, jnp.max(jnp.where(mask, scores, -1.0), axis=0, keepdims=True))

    score_send[...] = jnp.concatenate(list(split3(best)) + [jnp.zeros((5, held), f32)], axis=0)
    back_copies = []
    for k in range(1, n_dest):
        to = column_at(k)
        copy = remote(score_send.at[:, block(to)], back.at[:, block(me)],
                      back_ssem.at[k], back_rsem.at[k], device(to, rep))
        copy.start()
        back_copies.append(copy)
    back[:, block(me)] = score_send[:, block(me)]
    for copy in back_copies:
        copy.wait()
    mine = jnp.dot(back[...].astype(bf16), place_hot[...], preferred_element_type=f32)
    out[...] = mine[0:1, :] + mine[1:2, :] + mine[2:3, :]


def per_device(emb, basis, labels, owner_map, order):
    n_feat = lax.axis_size("feat")
    n_dest = lax.axis_size("owners") * n_feat
    row_dev = labels.shape[0]
    depth, width = basis.shape
    cap = 2 * row_dev // n_dest
    nclust = owner_map.shape[0]
    fits = (
        n_feat == 2 and lax.axis_size("rep") == 2 and cap % LANES == 0 and width == 2 * LANES
        and row_dev % (16 * CHUNKS) == 0 and nclust == 8 * n_dest and lax.axis_size("owners") == 4
    )
    if not fits:
        return per_device_plain(emb, basis, labels, owner_map, order)
    held = n_dest * cap
    n_col = width // LANES
    dma = pltpu.SemaphoreType.DMA
    vmem = pl.BlockSpec(memory_space=pltpu.VMEM)
    hbm = pl.BlockSpec(memory_space=pltpu.HBM)
    best = pl.pallas_call(
        functools.partial(window_kernel, n_dest, n_feat, cap),
        out_shape=jax.ShapeDtypeStruct((1, row_dev), jnp.float32),
        in_specs=[hbm] * 5,
        out_specs=vmem,
        scratch_shapes=[
            pltpu.VMEM((1, row_dev), jnp.int32),
            pltpu.VMEM((1, nclust), jnp.int32),
            pltpu.VMEM((1, row_dev), jnp.int32),
            pltpu.VMEM((n_feat * row_dev, depth), jnp.bfloat16),
            pltpu.VMEM((depth, width), jnp.bfloat16),
            pltpu.VMEM((row_dev, width), jnp.float32),
            pltpu.VMEM((row_dev, width), jnp.bfloat16),
            pltpu.VMEM((row_dev, width), jnp.bfloat16),
            pltpu.VMEM((held, row_dev), jnp.bfloat16),
            pltpu.VMEM((held, width), jnp.bfloat16),
            pltpu.VMEM((8, held), jnp.float32),
            pltpu.VMEM((2, 8, held), jnp.float32),
            pltpu.VMEM((2, held, width), jnp.bfloat16),
            pltpu.VMEM((2, held, width), jnp.bfloat16),
            pltpu.VMEM((8, held), jnp.float32),
            pltpu.VMEM((8, held), jnp.float32),
            pltpu.SemaphoreType.REGULAR((CHUNKS,)),
            dma((2 * CHUNKS + 4,)),
            dma((CHUNKS + n_col - 1,)),
            dma((CHUNKS + n_col - 1,)),
            dma((n_dest,)),
            dma((n_dest,)),
            dma((n_col, n_dest)),
            dma((n_col, n_dest)),
            dma((n_col, n_dest)),
            dma((n_col, n_dest)),
            dma((n_dest,)),
            dma((n_dest,)),
        ],
        compiler_params=pltpu.CompilerParams(
            collective_id=0, has_side_effects=True, vmem_limit_bytes=60 * 1024 * 1024
        ),
        name="dedup_window",
    )(emb, basis, labels.reshape(1, row_dev), owner_map.reshape(1, nclust), order.reshape(1, row_dev))
    return best.reshape(row_dev)


def solution(mesh):
    return jax.shard_map(
        per_device,
        mesh=mesh,
        in_specs=(
            P(("groups", "owners", "rep"), "feat"),
            P("feat", None),
            P(("groups", "owners", "rep", "feat")),
            P("groups"),
            P(("groups", "owners", "rep", "feat")),
        ),
        out_specs=P(("groups", "owners", "rep", "feat")),
        check_vma=False,
    )
```

```python
import functools

import jax
import jax.numpy as jnp
from jax import lax
from jax.experimental import pallas as pl
from jax.experimental.pallas import tpu as pltpu
from jax.sharding import PartitionSpec as P


def unitize(diff):
    scale = lax.rsqrt(jnp.mean(diff * diff, axis=-1, keepdims=True) + 1e-06)
    return (diff * scale / jnp.sqrt(jnp.float32(diff.shape[-1]))).astype(jnp.bfloat16)


def per_device_plain(emb, basis, labels, owner_map, order):
    row_dev = labels.shape[0]
    width = basis.shape[1]
    n_own = lax.axis_size("owners")
    n_col = lax.axis_size("feat")
    n_dest = n_own * n_col
    nclust = owner_map.shape[0]
    cl_dest = nclust // n_dest
    cap = 2 * row_dev // n_dest
    proj = lax.psum_scatter(
        jnp.dot(emb, basis, preferred_element_type=jnp.float32),
        "feat",
        scatter_dimension=0,
        tiled=True,
    ).astype(jnp.bfloat16)
    cluster_ids = jnp.arange(nclust, dtype=jnp.int32)
    slot = jnp.sum(
        jnp.where(labels[:, None] == cluster_ids[None, :], owner_map[None, :], 0), axis=1
    )
    dest = slot // cl_dest
    dest_hot = (dest[:, None] == jnp.arange(n_dest, dtype=jnp.int32)[None, :]).astype(jnp.int32)
    rank = jnp.sum(jnp.cumsum(dest_hot, axis=0) * dest_hot, axis=1) - 1
    place = dest * cap + rank
    member = (slot[:, None] == cluster_ids[None, :]).astype(jnp.bfloat16)
    sums = lax.dot_general(
        member, proj, (((0,), (0,)), ((), ())), preferred_element_type=jnp.float32
    )
    counts = jnp.sum(member.astype(jnp.float32), axis=0)
    all_sums, all_counts = lax.psum((sums, counts), ("owners", "feat", "rep"))
    centre = jnp.take(all_sums, slot, axis=0) / jnp.take(all_counts, slot)[:, None]
    payload = unitize(proj.astype(jnp.float32) - centre)
    vec_buf = jnp.zeros((n_dest * cap, width), jnp.bfloat16).at[place].set(payload)
    slot_buf = jnp.full((n_dest * cap,), -1, jnp.int32).at[place].set(slot)
    order_buf = jnp.zeros((n_dest * cap,), jnp.int32).at[place].set(order)
    got_vec, got_slot, got_order = (
        lax.all_to_all(
            vec_buf.reshape(n_dest, cap, width),
            ("owners", "feat"),
            split_axis=0,
            concat_axis=0,
            tiled=True,
        ),
        lax.all_to_all(
            slot_buf.reshape(n_dest, cap),
            ("owners", "feat"),
            split_axis=0,
            concat_axis=0,
            tiled=True,
        ),
        lax.all_to_all(
            order_buf.reshape(n_dest, cap),
            ("owners", "feat"),
            split_axis=0,
            concat_axis=0,
            tiled=True,
        ),
    )
    held = n_dest * cap
    got_vec = got_vec.reshape(held, width)
    got_slot = got_slot.reshape(held)
    got_order = got_order.reshape(held)
    start_best = jnp.full((held,), -1.0, jnp.float32)
    keys = lax.all_gather(got_vec, "rep", axis=0, tiled=True)
    key_slot = lax.all_gather(got_slot, "rep", axis=0, tiled=True)
    key_order = lax.all_gather(got_order, "rep", axis=0, tiled=True)
    scores = lax.dot_general(
        got_vec, keys, (((1,), (1,)), ((), ())), preferred_element_type=jnp.float32
    )
    mask = (
        (got_slot[:, None] == key_slot[None, :])
        & (key_order[None, :] < got_order[:, None])
        & (key_slot[None, :] >= 0)
    )
    found = jnp.maximum(start_best, jnp.max(jnp.where(mask, scores, jnp.float32(-1.0)), axis=1))
    back = lax.all_to_all(
        found.reshape(n_dest, cap), ("owners", "feat"), split_axis=0, concat_axis=0, tiled=True
    )
    return jnp.take(back.reshape(held), place)


LANES = 128
CHUNKS = 4


def split3(v):
    hi = v.astype(jnp.bfloat16).astype(jnp.float32)
    mid = (v - hi).astype(jnp.bfloat16).astype(jnp.float32)
    return hi, mid, v - hi - mid


def window_kernel(
    n_dest, n_feat, cap,
    emb, basis, labels_h, owner_map_h, order_h, out,
    labels, owner_map, order, emb_v, basis_v, own, part_send, part_recv, place_hot, buf, meta_send, meta, rows, unit,
    score_send, back,
    near_sem, load_sem, part_ssem, part_rsem, meta_ssem, meta_rsem, vec_ssem, vec_rsem,
    fwd_ssem, fwd_rsem, back_ssem, back_rsem,
):
    f32, bf16 = jnp.float32, jnp.bfloat16
    half = part_send.shape[0]
    width = part_send.shape[1]
    held = n_dest * cap
    step = half // CHUNKS
    n_col = width // LANES
    nclust = owner_map.shape[1]
    cl_dest = nclust // n_dest
    feat = lax.axis_index("feat")
    rep = lax.axis_index("rep")
    me = lax.axis_index("owners") * n_feat + feat
    other = 1 - rep

    def device(column, r):
        return {"owners": column // n_feat, "feat": column % n_feat, "rep": r}

    def column_at(k):
        return lax.rem(me + k, n_dest)

    def block(column):
        return pl.ds(pl.multiple_of(column * cap, cap), cap)

    def remote(src, dst, ssem, rsem, to):
        return pltpu.make_async_remote_copy(
            src_ref=src, dst_ref=dst, send_sem=ssem, recv_sem=rsem,
            device_id=to, device_id_type=pl.DeviceIdType.MESH,
        )

    barrier = pltpu.get_barrier_semaphore()
    owner = lax.axis_index("owners")
    n_own = n_dest // n_feat
    low, high = owner > 0, owner < n_own - 1
    n_near = 1 + low.astype(jnp.int32) + high.astype(jnp.int32)

    def greet(sem):
        def signal(to):
            pl.semaphore_signal(sem, inc=1, device_id=to, device_id_type=pl.DeviceIdType.MESH)

        signal({"feat": 1 - feat})

        @pl.when(low)
        def _():
            signal({"owners": owner - 1})

        @pl.when(high)
        def _():
            signal({"owners": owner + 1})

    greet(barrier)
    pl.semaphore_signal(barrier, inc=1, device_id={"rep": other}, device_id_type=pl.DeviceIdType.MESH)

    small = [pltpu.make_async_copy(h, v, load_sem.at[2 * CHUNKS + 1 + i]) for i, (h, v) in enumerate(
        ((labels_h, labels), (owner_map_h, owner_map), (order_h, order)))]
    loads = [pltpu.make_async_copy(basis, basis_v, load_sem.at[2 * CHUNKS])]
    for c in range(2 * CHUNKS):
        side = 1 - feat if c < CHUNKS else feat
        at = pl.multiple_of(side * half + (c % CHUNKS) * step, step)
        loads.append(pltpu.make_async_copy(
            emb.at[pl.ds(at, step), :], emb_v.at[pl.ds(c * step, step), :], load_sem.at[c]))
    for load in small + loads:
        load.start()

    peer = {"feat": 1 - feat}
    part_copies = [[], []]
    loads[0].wait()
    for c in range(CHUNKS):
        at = pl.ds(c * step, step)
        loads[1 + c].wait()
        part_send[at, :] = jnp.dot(
            emb_v[at, :], basis_v[...], preferred_element_type=f32).astype(bf16)
        if c == 0:
            pl.semaphore_wait(barrier, 1 + n_near)
            greet(near_sem.at[0])
        cut = (at, pl.ds(0, LANES))
        copy = remote(part_send.at[cut], part_recv.at[cut], part_ssem.at[c], part_rsem.at[c], peer)
        copy.start()
        part_copies[0].append(copy)
    for n in range(1, n_col):
        cut = (slice(None), pl.ds(n * LANES, LANES))
        copy = remote(part_send.at[cut], part_recv.at[cut], part_ssem.at[CHUNKS + n - 1],
                      part_rsem.at[CHUNKS + n - 1], peer)
        copy.start()
        part_copies[n].append(copy)

    def hear(c):
        pl.semaphore_wait(near_sem.at[c], n_near)
        if c < n_own - 2:
            greet(near_sem.at[c + 1])

    for load in small:
        load.wait()
    omap = owner_map[...].astype(f32)
    eye = (lax.broadcasted_iota(jnp.int32, (nclust, nclust), 0)
           == lax.broadcasted_iota(jnp.int32, (nclust, nclust), 1))
    omap_col = jnp.sum(jnp.where(eye, omap, 0.0), axis=1, keepdims=True)
    label_hot = lax.broadcasted_iota(jnp.int32, (nclust, half), 0) == labels[...]
    slot = jnp.sum(jnp.where(label_hot, omap_col, 0.0), axis=0, keepdims=True)
    dest = jnp.floor(slot * (1.0 / cl_dest))
    local = slot - dest * cl_dest
    dest_hot = lax.broadcasted_iota(jnp.int32, (n_dest, half), 0) == dest.astype(jnp.int32)
    upto = (lax.broadcasted_iota(jnp.int32, (half, half), 0)
            <= lax.broadcasted_iota(jnp.int32, (half, half), 1))
    running = jnp.dot(
        jnp.where(dest_hot, 1.0, 0.0).astype(bf16), jnp.where(upto, 1.0, 0.0).astype(bf16),
        preferred_element_type=f32)
    rank = jnp.sum(jnp.where(dest_hot, running, 0.0), axis=0, keepdims=True) - 1.0
    place = (dest * cap + rank).astype(jnp.int32)

    hear(0)

    place_hot[...] = jnp.where(
        lax.broadcasted_iota(jnp.int32, (held, half), 0) == place, 1.0, 0.0).astype(bf16)
    ranks = order[...]
    pieces = jnp.concatenate([
        local + 1.0,
        lax.shift_right_logical(ranks, 14).astype(f32),
        (lax.shift_right_logical(ranks, 7) & 127).astype(f32),
        (ranks & 127).astype(f32),
        jnp.zeros((4, half), f32)], axis=0).astype(bf16)
    placed = lax.dot_general(pieces, place_hot[...], (((1,), (1,)), ((), ())),
                             preferred_element_type=f32)
    meta_send[...] = jnp.zeros_like(meta_send)
    meta_send[0:1, :] = placed[0:1, :]
    meta_send[1:2, :] = placed[1:2, :] * 16384.0 + placed[2:3, :] * 128.0 + placed[3:4, :]
    hear(1)

    for c in range(CHUNKS):
        at = pl.ds(c * step, step)
        loads[1 + CHUNKS + c].wait()
        own[at, :] = jnp.dot(
            emb_v[pl.ds((CHUNKS + c) * step, step), :], basis_v[...], preferred_element_type=f32)

    hear(2)
    meta_copies = [None]
    for k in range(1, n_dest):
        to = column_at(k)
        copy = remote(meta_send.at[:, block(to)], meta.at[0, :, block(me)],
                      meta_ssem.at[k], meta_rsem.at[k], device(to, rep))
        copy.start()
        meta_copies.append(copy)
    meta[0, :, block(me)] = meta_send[:, block(me)]

    side = owner // (n_own // 2)
    ways = [(o, x) for o in (3 * (1 - side), 2 - side, 4 * side + 1 - owner, owner) for x in (feat, 1 - feat)]
    ways = ways[:-2] + [ways[-1]]
    vec_copies = [[None] * n_dest for _ in range(n_col)]
    for n in range(n_col):
        lanes = pl.ds(n * LANES, LANES)
        for copy in part_copies[n]:
            copy.wait_recv()
        proj = (own[:, lanes] + part_recv[:, lanes].astype(f32)).astype(bf16)

        def put(column):
            buf[block(column), lanes] = jnp.dot(
                place_hot[block(column), :], proj, preferred_element_type=f32).astype(bf16)

        def send(to, k):
            return remote(buf.at[block(to), lanes], rows.at[0, block(me), lanes],
                          vec_ssem.at[n, k], vec_rsem.at[n, k], device(to, rep))

        for o, x in ways:
            to = o * n_feat + x
            put(to)
            send(to, lax.rem(to - me + n_dest, n_dest)).start()
        for k in range(1, n_dest):
            vec_copies[n][k] = send(column_at(k), k)
        put(me)
        rows[0, block(me), lanes] = buf[block(me), lanes]
    for copies in part_copies:
        for copy in copies:
            copy.wait_send()

    for copy in meta_copies[1:]:
        copy.wait()
    copy = remote(meta.at[0], meta.at[1], meta_ssem.at[0], meta_rsem.at[0], {"rep": other})
    copy.start()
    copy.wait()
    member = lax.broadcasted_iota(jnp.int32, (8, held), 0).astype(f32) + 1.0
    hot = [jnp.where(meta[r, 0:1, :] == member, 1.0, 0.0) for r in range(2)]
    counts = jnp.sum(hot[0], axis=1, keepdims=True) + jnp.sum(hot[1], axis=1, keepdims=True)
    hot = [h.astype(bf16) for h in hot]

    fwd_copies = []
    for n in range(n_col):
        lanes = pl.ds(n * LANES, LANES)
        for k in range(n_dest):
            came = lax.rem(me + n_dest - k, n_dest)
            if k:
                vec_copies[n][k].wait_recv()
            copy = remote(rows.at[0, block(came), lanes], rows.at[1, block(came), lanes],
                          fwd_ssem.at[n, k], fwd_rsem.at[n, k], {"rep": other})
            copy.start()
            fwd_copies.append(copy)
    sums = jnp.dot(hot[0], rows[0], preferred_element_type=f32)
    for copies in vec_copies:
        for copy in copies[1:]:
            copy.wait_send()
    cols = [jnp.transpose(meta[r]) for r in range(2)]
    for copy in fwd_copies:
        copy.wait()
    sums = sums + jnp.dot(hot[1], rows[1], preferred_element_type=f32)

    centre = jnp.where(counts > 0.0, sums / jnp.maximum(counts, 1.0), 0.0)
    centre3 = jnp.concatenate(
        list(split3(centre)) + [jnp.zeros((LANES - 24, width), f32)], axis=0).astype(bf16)
    lane = lax.broadcasted_iota(jnp.int32, (held, LANES), 1)
    want = jnp.where(lane < 24, (lane & 7) + 1, -1).astype(f32)
    for r in range(2):
        hot_col = jnp.where(cols[r][:, 0:1] == want, 1.0, 0.0).astype(bf16)
        diff = rows[r].astype(f32) - jnp.dot(hot_col, centre3, preferred_element_type=f32)
        mean = jnp.sum(diff * diff, axis=-1, keepdims=True) * (1.0 / width)
        scale = lax.rsqrt(mean + 1e-06)
        unit[r, :, :] = (diff * scale / jnp.sqrt(f32(width))).astype(bf16)

    my_slot, my_order = meta[0, 0:1, :], meta[0, 1:2, :]
    best = jnp.full((1, held), -1.0, f32)
    tile = 256 if held % 256 == 0 else cap
    for r in range(2):
        from_slot = jnp.where(cols[r][:, 0:1] > 0.0, cols[r][:, 0:1], -5.0)
        from_order = cols[r][:, 1:2]
        for t in range(held // tile):
            cut = slice(t * tile, (t + 1) * tile)
            scores = lax.dot_general(unit[r, cut, :], unit[0], (((1,), (1,)), ((), ())),
                                     preferred_element_type=f32)
            mask = (from_slot[cut] == my_slot) & (from_order[cut] < my_order)
            best = jnp.maximum(best, jnp.max(jnp.where(mask, scores, -1.0), axis=0, keepdims=True))

    score_send[...] = jnp.concatenate(list(split3(best)) + [jnp.zeros((5, held), f32)], axis=0)
    back_copies = []
    for k in range(1, n_dest):
        to = column_at(k)
        copy = remote(score_send.at[:, block(to)], back.at[:, block(me)],
                      back_ssem.at[k], back_rsem.at[k], device(to, rep))
        copy.start()
        back_copies.append(copy)
    back[:, block(me)] = score_send[:, block(me)]
    for copy in back_copies:
        copy.wait()
    mine = jnp.dot(back[...].astype(bf16), place_hot[...], preferred_element_type=f32)
    out[...] = mine[0:1, :] + mine[1:2, :] + mine[2:3, :]


def per_device(emb, basis, labels, owner_map, order):
    n_feat = lax.axis_size("feat")
    n_dest = lax.axis_size("owners") * n_feat
    row_dev = labels.shape[0]
    depth, width = basis.shape
    cap = 2 * row_dev // n_dest
    nclust = owner_map.shape[0]
    fits = (
        n_feat == 2 and lax.axis_size("rep") == 2 and cap % LANES == 0 and width == 2 * LANES
        and row_dev % (16 * CHUNKS) == 0 and nclust == 8 * n_dest and lax.axis_size("owners") == 4
    )
    if not fits:
        return per_device_plain(emb, basis, labels, owner_map, order)
    held = n_dest * cap
    n_col = width // LANES
    dma = pltpu.SemaphoreType.DMA
    vmem = pl.BlockSpec(memory_space=pltpu.VMEM)
    hbm = pl.BlockSpec(memory_space=pltpu.HBM)
    best = pl.pallas_call(
        functools.partial(window_kernel, n_dest, n_feat, cap),
        out_shape=jax.ShapeDtypeStruct((1, row_dev), jnp.float32),
        in_specs=[hbm] * 5,
        out_specs=vmem,
        scratch_shapes=[
            pltpu.VMEM((1, row_dev), jnp.int32),
            pltpu.VMEM((1, nclust), jnp.int32),
            pltpu.VMEM((1, row_dev), jnp.int32),
            pltpu.VMEM((n_feat * row_dev, depth), jnp.bfloat16),
            pltpu.VMEM((depth, width), jnp.bfloat16),
            pltpu.VMEM((row_dev, width), jnp.float32),
            pltpu.VMEM((row_dev, width), jnp.bfloat16),
            pltpu.VMEM((row_dev, width), jnp.bfloat16),
            pltpu.VMEM((held, row_dev), jnp.bfloat16),
            pltpu.VMEM((held, width), jnp.bfloat16),
            pltpu.VMEM((8, held), jnp.float32),
            pltpu.VMEM((2, 8, held), jnp.float32),
            pltpu.VMEM((2, held, width), jnp.bfloat16),
            pltpu.VMEM((2, held, width), jnp.bfloat16),
            pltpu.VMEM((8, held), jnp.float32),
            pltpu.VMEM((8, held), jnp.float32),
            pltpu.SemaphoreType.REGULAR((CHUNKS,)),
            dma((2 * CHUNKS + 4,)),
            dma((CHUNKS + n_col - 1,)),
            dma((CHUNKS + n_col - 1,)),
            dma((n_dest,)),
            dma((n_dest,)),
            dma((n_col, n_dest)),
            dma((n_col, n_dest)),
            dma((n_col, n_dest)),
            dma((n_col, n_dest)),
            dma((n_dest,)),
            dma((n_dest,)),
        ],
        compiler_params=pltpu.CompilerParams(
            collective_id=0, has_side_effects=True, vmem_limit_bytes=60 * 1024 * 1024
        ),
        name="dedup_window",
    )(emb, basis, labels.reshape(1, row_dev), owner_map.reshape(1, nclust), order.reshape(1, row_dev))
    return best.reshape(row_dev)


def solution(mesh):
    return jax.shard_map(
        per_device,
        mesh=mesh,
        in_specs=(
            P(("groups", "owners", "rep"), "feat"),
            P("feat", None),
            P(("groups", "owners", "rep", "feat")),
            P("groups"),
            P(("groups", "owners", "rep", "feat")),
        ),
        out_specs=P(("groups", "owners", "rep", "feat")),
        check_vma=False,
    )
```
